32 devices in a mesh: groups: 2 (over y), wide: 4 (over z), narrow: 4 (over x, core).
Axes of the slice: x: 2, y: 2, z: 4, core: 2. Of those that a mesh axis runs over, the one named last changes fastest.
Arguments:
- inputs: bfloat16 [2, 64, 16384], P(None, 'groups', 'wide'), parts along dimension 1, may hold values from -6 to 6
- w_qkv: bfloat16 [16384, 14336], P('wide', 'narrow'), may hold values from -0.046875 to 0.046875
- w_out: bfloat16 [12288, 16384], P('narrow', 'wide'), may hold values from -0.21875 to 0.21875
- key_cache: bfloat16 [64, 8, 256, 128], P(('groups', 'wide'), 'narrow'), parts along dimension 0, may hold values from -9 to 9
- value_cache: bfloat16 [64, 8, 256, 128], P(('groups', 'wide'), 'narrow'), parts along dimension 0, may hold values from -6 to 6
- positions: int32 [64], P(('groups', 'wide')), parts along dimension 0, may hold values from 0 to 8191
- lengths: int32 [64], P(('groups', 'wide')), parts along dimension 0, may hold values from 1 to 256, as said below
Outputs:
- attended: bfloat16 [2, 64, 16384], P(None, ('groups', 'narrow'), 'wide'), parts along dimension 1
The draws below stay inside these ranges and needn't reach their ends.
There are 2 independent parts, one for each index of `groups`. The reference program is written for one: setup_inputs(seed, part) draws one part's arguments, and reference() takes and returns one part's arrays. A program takes and returns all parts, laid end to end along the dimension named above; an argument that names none is the same for every part. Nothing has to cross between parts.
Inputs may be any that keep to these rules, and one draw needn't show every extreme that they name: `lengths`: at least one row has all 256 slots valid.
All inputs are finite; a program needn't handle non-finite values.
Results may differ from the reference program's by a relative error of at most 0.025.
Values may be sent and summed in bfloat16 or wider, within the bound.
A program may use at most 128 MiB of HBM per device.

```python
import jax
import jax.numpy as jnp
from jax import lax

D = 16384
KVH = 8
HD = 128
G = 12
CACHE = 256
HQ = 96
ROWS = 32
N_NARROW = 4


def draw_lengths(key, part):
    key = jax.random.fold_in(key, 7)
    first_key, second_key = jax.random.split(key)
    drawn = jax.random.randint(first_key, (ROWS,), 1, CACHE + 1)
    chosen = jax.random.randint(second_key, (), 0, ROWS)
    return jnp.where(jnp.arange(ROWS) == chosen, CACHE, drawn).astype(jnp.int32)


def with_ends(array, stream_key, least, largest):
    longest = array.shape.index(max(array.shape))
    spots = []
    for shift in (0, 1):
        where = [jax.random.randint(jax.random.fold_in(stream_key, axis), (), 0, length) for axis, length in enumerate(array.shape)]
        where[longest] = (where[longest] + shift) % array.shape[longest]
        spots.append(tuple(where))
    return array.at[spots[0]].set(least).at[spots[1]].set(largest)


def level_of(rng, dims, pieces, smallest, top_value):
    factor_of, own = 1.0, jax.random.fold_in(rng, 6)
    for dim, blocks in pieces:
        draws = jnp.exp(jax.random.uniform(jax.random.fold_in(own, dim), (blocks,), jnp.float32, smallest / len(pieces), top_value / len(pieces)))
        factor_of = factor_of * jnp.repeat(draws, dims[dim] // blocks).reshape([-1 if axis == dim else 1 for axis in range(len(dims))])
    return factor_of


def centred(key, extent, spread, bound, pieces=(), kind=jnp.bfloat16):
    values = jax.random.normal(key, extent, jnp.float32) * spread
    if len(pieces) > 0:
        values = level_of(key, extent, pieces, -0.22, 0.18) * values
    return jnp.clip(values, min=-bound, max=bound).astype(kind)


def setup_inputs(seed: int = 0, part: int = 0) -> dict:
    splits = jax.random.split(jax.random.key(seed), 8)
    part_keys = jax.random.split(jax.random.fold_in(splits[7], part), 8)
    return {
        "inputs": centred(part_keys[0], (2, ROWS, D), 1.0, 6.0, ((2, 4),)),
        "w_qkv": centred(splits[1], (D, KVH * (G + 2) * HD), D ** -0.5, 0.046875, ((0, 4), (1, 4))),
        "w_out": centred(splits[2], (HQ * HD, D), (HQ * HD // 16) ** -0.5, 0.21875, ((0, 4), (1, 4))),
        "key_cache": centred(part_keys[3], (ROWS, KVH, CACHE, HD), 1.5, 9.0, ((0, 4), (1, 4))),
        "value_cache": centred(part_keys[4], (ROWS, KVH, CACHE, HD), 1.0, 6.0, ((0, 4), (1, 4))),
        "positions": with_ends(jax.random.randint(part_keys[5], (ROWS,), 0, 8192), jax.random.fold_in(part_keys[5], 1), 0, 8191).astype(jnp.int32),
        "lengths": draw_lengths(jax.random.fold_in(jax.random.fold_in(splits[7], part), 71), part),
    }


def rotary(values_in, position_now):
    half_size = values_in.shape[-1] // 2
    inverse_freq = 500000.0 ** (-(jnp.arange(half_size, dtype=jnp.float32) * 2.0 / values_in.shape[-1]))
    angles = position_now.astype(jnp.float32)[..., None] * inverse_freq
    cosine = jnp.cos(angles)
    sine_val = jnp.sin(angles)
    first_half = values_in[..., :half_size]
    second_half = values_in[..., half_size:]
    return jnp.concatenate([first_half * cosine - second_half * sine_val, second_half * cosine + first_half * sine_val], axis=-1)


def reference(inputs, w_qkv, w_out, key_cache, value_cache, positions, lengths):
    score_scale = HD ** -0.5
    valid_keys = jnp.arange(CACHE)[None, :] < lengths[:, None]
    cached_keys = key_cache.astype(jnp.float32)
    cached_values = value_cache.astype(jnp.float32)
    new_keys = []
    new_values = []
    results = []
    block_cols = HQ * HD // N_NARROW
    for step_index in range(2):
        joined = jnp.dot(inputs[step_index], w_qkv, preferred_element_type=jnp.float32).reshape(ROWS, KVH, G + 2, HD)
        position_now = positions + step_index
        query_new = rotary(joined[:, :, :G], position_now[:, None, None]).astype(jnp.bfloat16)
        key_new = rotary(joined[:, :, G], position_now[:, None]).astype(jnp.bfloat16)
        value_new = joined[:, :, G + 1].astype(jnp.bfloat16)
        new_keys.append(key_new.astype(jnp.float32))
        new_values.append(value_new.astype(jnp.float32))
        query_f = query_new.astype(jnp.float32)
        cache_scores = jnp.einsum("rhgd,rhjd->rhgj", query_f, cached_keys) * score_scale
        fresh_scores = jnp.einsum("rhgd,trhd->rhgt", query_f, jnp.stack(new_keys)) * score_scale
        cache_exp = jnp.where(valid_keys[:, None, None, :], jnp.exp(cache_scores), jnp.float32(0.0))
        fresh_exp = jnp.exp(fresh_scores)
        denominator = jnp.sum(cache_exp, axis=-1) + jnp.sum(fresh_exp, axis=-1)
        cache_weights = (cache_exp / denominator[..., None]).astype(jnp.bfloat16).astype(jnp.float32)
        fresh_weights = (fresh_exp / denominator[..., None]).astype(jnp.bfloat16).astype(jnp.float32)
        heads = jnp.einsum("rhgj,rhjd->rhgd", cache_weights, cached_values)
        heads = heads + jnp.einsum("rhgt,trhd->rhgd", fresh_weights, jnp.stack(new_values))
        heads = heads.astype(jnp.bfloat16).reshape(ROWS, HQ * HD)
        summed = jnp.zeros((ROWS, D), jnp.float32)
        for block_index in range(N_NARROW):
            lower = block_index * block_cols
            partial_term = jnp.dot(heads[:, lower:lower + block_cols], w_out[lower:lower + block_cols], preferred_element_type=jnp.float32)
            rounded = lax.optimization_barrier(partial_term.astype(jnp.bfloat16))
            summed = summed + rounded.astype(jnp.float32)
        results.append(summed.astype(jnp.bfloat16))
    return jnp.stack(results)
```

```python
import functools

import jax
import jax.numpy as jnp
import numpy as np
from jax import lax
from jax.experimental import pallas as pl
from jax.experimental.pallas import tpu as pltpu
from jax.sharding import PartitionSpec as P

MESH = pl.DeviceIdType.MESH
F32 = jnp.float32
BF16 = jnp.bfloat16


def layer_kernel(
    s,
    pos_ref, len_ref, freq_ref, x_hbm, wq_hbm, wo_hbm, kc_hbm, vc_hbm,
    out_ref,
    x_v, wq_v, wo_v, kc_v, vc_v,
    qsend, qrecv, heads_v, acc, psend, precv, qs, os,
    x_sem, kv_sem, wq_sem, wo_sem,
    qsend_sem, qrecv_sem, gsend_sem, grecv_sem, psend_sem, precv_sem,
):
    nw, nn = s["nw"], s["nn"]
    H, G, HD = s["H"], s["G"], s["HD"]
    R = s["R"]
    C, NC, B = s["C"], s["NC"], s["B"]
    C2, NP = s["C2"], s["NP"]
    HK = G * HD
    GP = s["GP"]
    slots = s["slots"]
    q = nw // nn
    total = H * NC
    pieces = H * NP
    scale = HD ** -0.5
    me = lax.axis_index("wide")
    me_n = lax.axis_index("narrow")

    def wide_at(d):
        return lax.rem(me + d, nw)

    def narrow_at(d):
        return lax.rem(me_n + d, nn)

    def wq_copy(i):
        slot = lax.rem(i, B)
        return pltpu.make_async_copy(
            wq_hbm.at[:, pl.ds(pl.multiple_of(i * C, C), C)], wq_v.at[slot], wq_sem.at[slot]
        )

    def wo_copy(i):
        h, c = i // NP, lax.rem(i, NP)
        return pltpu.make_async_copy(
            wo_hbm.at[pl.ds(pl.multiple_of(h * HK, HK), HK), pl.ds(pl.multiple_of(c * C2, C2), C2)],
            wo_v.at[i],
            wo_sem.at[i],
        )

    x_copy = pltpu.make_async_copy(x_hbm, x_v, x_sem)
    k_copy = pltpu.make_async_copy(kc_hbm, kc_v, kv_sem.at[0])
    v_copy = pltpu.make_async_copy(vc_hbm, vc_v, kv_sem.at[1])
    x_copy.start()
    for i in range(B):
        wq_copy(jnp.int32(i)).start()
    k_copy.start()
    v_copy.start()

    barrier = pltpu.get_barrier_semaphore()
    for d in range(1, nw):
        pl.semaphore_signal(barrier, inc=1, device_id={"wide": wide_at(d)}, device_id_type=MESH)
    for d in range(1, nn):
        pl.semaphore_signal(barrier, inc=1, device_id={"narrow": narrow_at(d)}, device_id_type=MESH)

    row_id = lax.broadcasted_iota(jnp.int32, (R, HD), 0)
    place = jnp.zeros((R, HD), jnp.int32)
    for r in range(R):
        place = jnp.where(row_id == r, pos_ref[r], place)
    freq = jnp.broadcast_to(freq_ref[...], (R, HD))
    lane = lax.broadcasted_iota(jnp.int32, (2 * R, HD), 1)
    angles = jnp.concatenate([place.astype(F32) * freq, (place + 1).astype(F32) * freq], axis=0)
    cosine = jnp.cos(angles)
    sine = jnp.sin(angles)
    sine = jnp.where(lane < HD // 2, -sine, sine)
    qs[...] = jnp.zeros_like(qs)

    pl.semaphore_wait(barrier, nw + nn - 2)
    x_copy.wait()

    def chunk(i, h):
        c = i - h * NC
        wq_copy(i).wait()
        slot = lax.rem(i, B)
        got = jnp.dot(
            x_v[...].reshape(2 * nw * R, x_v.shape[-1]), wq_v[slot], preferred_element_type=F32
        )
        half = nw * R
        for p in range(nw):
            qsend[h, p, c] = jnp.concatenate(
                [got[p * R:(p + 1) * R], got[half + p * R:half + (p + 1) * R]], axis=0
            ).astype(BF16)
        for d in range(1, nw):
            to = wide_at(d)
            pltpu.make_async_remote_copy(
                src_ref=qsend.at[h, to, c],
                dst_ref=qrecv.at[h, me, c],
                send_sem=qsend_sem.at[h, d],
                recv_sem=qrecv_sem.at[h, d],
                device_id={"wide": to},
                device_id_type=MESH,
            ).start()

        @pl.when(i + B < total)
        def _():
            wq_copy(i + B).start()

        @pl.when((i + B >= total) & (i + B - total < pieces))
        def _():
            wo_copy(i + B - total).start()

    def chunks(h, lo, hi):
        def body(i, carry):
            chunk(i, h)
            return carry

        lax.fori_loop(h * NC + lo, h * NC + hi, body, 0)

    def attention(h):
        joined = qsend[h, me].astype(F32)
        for d in range(1, nw):
            src = lax.rem(me + nw - d, nw)
            pltpu.make_async_copy(qrecv.at[h, src], qrecv.at[h, src], qrecv_sem.at[h, d]).wait()
            joined = joined + qrecv[h, src].astype(F32)
        per = C // HD

        def entry(g):
            return joined[g // per][:, (g % per) * HD:(g % per + 1) * HD]

        def rotated(g):
            t = entry(g)
            t = t * cosine + pltpu.roll(t, HD // 2, 1) * sine
            return t.astype(BF16).astype(F32)

        for g in range(G):
            t = rotated(g)
            qs[:, g, :] = t[:R]
            qs[:, GP + g, :] = t[R:]
        key_new = rotated(G)
        value_new = entry(G + 1).astype(BF16).astype(F32)
        slot_id = lax.broadcasted_iota(jnp.int32, (2 * GP, slots), 1)
        second = lax.broadcasted_iota(jnp.int32, (2 * GP, 1), 0) >= GP
        for r in range(R):
            qr = qs[r]
            scores = lax.dot_general(
                qr.astype(BF16), kc_v[r, h], (((1,), (1,)), ((), ())), preferred_element_type=F32
            ) * scale
            e = jnp.where(slot_id < len_ref[r], jnp.exp(scores), 0.0)
            f0 = jnp.exp(jnp.sum(qr * key_new[r:r + 1], axis=1, keepdims=True) * scale)
            f1 = jnp.exp(jnp.sum(qr * key_new[R + r:R + r + 1], axis=1, keepdims=True) * scale)
            f1 = jnp.where(second, f1, 0.0)
            den = jnp.sum(e, axis=1, keepdims=True) + f0 + f1
            o = jnp.dot((e / den).astype(BF16), vc_v[r, h], preferred_element_type=F32)
            o = o + (f0 / den).astype(BF16).astype(F32) * value_new[r:r + 1]
            o = o + (f1 / den).astype(BF16).astype(F32) * value_new[R + r:R + r + 1]
            os[r] = o
        for g in range(G):
            heads_v[h, me, :, g * HD:(g + 1) * HD] = jnp.concatenate(
                [os[:, g, :], os[:, GP + g, :]], axis=0
            ).astype(BF16)
        for d in range(1, nw):
            pltpu.make_async_remote_copy(
                src_ref=heads_v.at[h, me],
                dst_ref=heads_v.at[h, me],
                send_sem=gsend_sem.at[h, d],
                recv_sem=grecv_sem.at[h, d],
                device_id={"wide": wide_at(d)},
                device_id_type=MESH,
            ).start()

    def project(h):
        for d in range(1, nw):
            src = lax.rem(me + nw - d, nw)
            pltpu.make_async_copy(heads_v.at[h, src], heads_v.at[h, src], grecv_sem.at[h, d]).wait()

        def body(c, carry):
            i = h * NP + c
            wo_copy(i).wait()
            got = jnp.dot(
                heads_v[h].reshape(nw * 2 * R, HK), wo_v[i], preferred_element_type=F32
            )
            if h > 0:
                got = got + acc[c]
            if h < H - 1:
                acc[c] = got
                return carry
            rows = q * 2 * R
            for n in range(nn):
                psend[n, c] = got[n * rows:(n + 1) * rows].astype(BF16)
            for d in range(1, nn):
                to = narrow_at(d)
                pltpu.make_async_remote_copy(
                    src_ref=psend.at[to, c],
                    dst_ref=precv.at[me_n, c],
                    send_sem=psend_sem.at[d],
                    recv_sem=precv_sem.at[d],
                    device_id={"narrow": to},
                    device_id_type=MESH,
                ).start()
            return carry

        lax.fori_loop(0, NP, body, 0)

    for h in range(H):
        cut = (NC + 1) // 2 if h > 0 else NC
        chunks(h, 0, cut)
        if h > 0:
            if h == 1:
                k_copy.wait()
                v_copy.wait()
            attention(h - 1)
            chunks(h, cut, NC)
    if H == 1:
        k_copy.wait()
        v_copy.wait()
    for i in range(min(B, pieces), pieces):
        wo_copy(jnp.int32(i)).start()
    attention(H - 1)
    for h in range(H):
        project(h)

    for d in range(1, nn):
        src = lax.rem(me_n + nn - d, nn)
        pltpu.make_async_copy(precv.at[src], precv.at[src], precv_sem.at[d]).wait()
    for c in range(NP):
        tot = psend[me_n, c].astype(F32)
        for d in range(1, nn):
            tot = tot + precv[narrow_at(d), c].astype(F32)
        for t in range(2):
            part = jnp.concatenate(
                [tot[(2 * k + t) * R:(2 * k + t + 1) * R] for k in range(q)], axis=0
            )
            out_ref[t, :, c * C2:(c + 1) * C2] = part.astype(BF16)

    for d in range(1, nw):
        for h in range(H):
            to = wide_at(d)
            pltpu.make_async_copy(qsend.at[h, to], qsend.at[h, to], qsend_sem.at[h, d]).wait()
            pltpu.make_async_copy(heads_v.at[h, me], heads_v.at[h, me], gsend_sem.at[h, d]).wait()
    for d in range(1, nn):
        to = narrow_at(d)
        pltpu.make_async_copy(psend.at[to], psend.at[to], psend_sem.at[d]).wait()


def on_device(nw, nn, inputs, w_qkv, w_out, key_cache, value_cache, positions, lengths):
    R, H, slots, HD = key_cache.shape
    G = w_qkv.shape[1] // (H * HD) - 2
    K = w_qkv.shape[0]
    N = w_out.shape[1]
    HK = G * HD
    C = 2 * HD
    NC = w_qkv.shape[1] // (H * C)
    C2 = min(N, 4 * HD)
    NP = N // C2
    B = min(8, H * NC)
    GP = -(-G // 8) * 8
    q = nw // nn
    s = dict(nw=nw, nn=nn, H=H, G=G, HD=HD, R=R, C=C, NC=NC, B=B, C2=C2, NP=NP, GP=GP, slots=slots)
    half = np.arange(HD // 2, dtype=np.float64)
    freq = (500000.0 ** (-2.0 * half / HD)).astype(np.float32)
    freq = jnp.asarray(np.concatenate([freq, freq])[None, :])
    rows = q * 2 * R
    any_spec = pl.BlockSpec(memory_space=pl.ANY)
    smem = pl.BlockSpec(memory_space=pltpu.SMEM)
    vmem = pl.BlockSpec(memory_space=pltpu.VMEM)
    dma = pltpu.SemaphoreType.DMA
    return pl.pallas_call(
        functools.partial(layer_kernel, s),
        out_shape=jax.ShapeDtypeStruct((2, q * R, N), BF16),
        in_specs=[smem, smem, vmem] + [any_spec] * 5,
        out_specs=vmem,
        scratch_shapes=[
            pltpu.VMEM(inputs.shape, BF16),
            pltpu.VMEM((B, K, C), BF16),
            pltpu.VMEM((H * NP, HK, C2), BF16),
            pltpu.VMEM(key_cache.shape, BF16),
            pltpu.VMEM(value_cache.shape, BF16),
            pltpu.VMEM((H, nw, NC, 2 * R, C), BF16),
            pltpu.VMEM((H, nw, NC, 2 * R, C), BF16),
            pltpu.VMEM((H, nw, 2 * R, HK), BF16),
            pltpu.VMEM((NP, nw * 2 * R, C2), F32),
            pltpu.VMEM((nn, NP, rows, C2), BF16),
            pltpu.VMEM((nn, NP, rows, C2), BF16),
            pltpu.VMEM((R, 2 * GP, HD), F32),
            pltpu.VMEM((R, 2 * GP, HD), F32),
            dma,
            dma((2,)),
            dma((B,)),
            dma((H * NP,)),
            dma((H, nw)),
            dma((H, nw)),
            dma((H, nw)),
            dma((H, nw)),
            dma((nn,)),
            dma((nn,)),
        ],
        compiler_params=pltpu.CompilerParams(
            collective_id=0, has_side_effects=True, vmem_limit_bytes=58 * 1024 * 1024
        ),
        cost_estimate=pl.CostEstimate(
            flops=4 * nw * R * (K * w_qkv.shape[1] + H * HK * N),
            bytes_accessed=2 * (w_qkv.size + w_out.size + 2 * key_cache.size),
            transcendentals=0,
        ),
    )(positions, lengths, freq, inputs, w_qkv, w_out, key_cache, value_cache)


def solution(mesh):
    placed = (
        P(None, "groups", "wide"),
        P("wide", "narrow"),
        P("narrow", "wide"),
        P(("groups", "wide"), "narrow", None, None),
        P(("groups", "wide"), "narrow", None, None),
        P(("groups", "wide")),
        P(("groups", "wide")),
    )
    return jax.shard_map(
        functools.partial(on_device, mesh.shape["wide"], mesh.shape["narrow"]),
        mesh=mesh,
        in_specs=placed,
        out_specs=P(None, ("groups", "narrow"), "wide"),
        check_vma=False,
    )
```

```python
import functools

import jax
import jax.numpy as jnp
import numpy as np
from jax import lax
from jax.experimental import pallas as pl
from jax.experimental.pallas import tpu as pltpu
from jax.sharding import PartitionSpec as P

MESH = pl.DeviceIdType.MESH
F32 = jnp.float32
BF16 = jnp.bfloat16


def reversed_bits(p, n):
    out, j = 0, 1
    while j < n:
        out = out * 2 + (p // j) % 2
        j *= 2
    return out


class Halving:
    def __init__(self, axis, n, cur, sends, recvs, send_sem, recv_sem):
        self.axis, self.n, self.cur = axis, n, cur
        self.sends, self.recvs = sends, recvs
        self.send_sem, self.recv_sem = send_sem, recv_sem
        self.stages = len(sends)
        self.me = lax.axis_index(axis)
        self.place = reversed_bits(self.me, n)

    def partner(self, k):
        return self.me + (1 - 2 * ((self.me // 2 ** k) % 2)) * 2 ** k

    def regions(self, k):
        size = self.n // 2 ** (k + 1)
        keep = (self.place // size) * size
        return size, keep, keep + (1 - 2 * ((self.me // 2 ** k) % 2)) * size

    def copy(self, k, i):
        return pltpu.make_async_remote_copy(
            src_ref=self.sends[k].at[i],
            dst_ref=self.recvs[k].at[i],
            send_sem=self.send_sem.at[k, i],
            recv_sem=self.recv_sem.at[k, i],
            device_id={self.axis: self.partner(k)},
            device_id_type=MESH,
        )

    def exchange(self, k, i):
        if k > 0:
            size, keep, _ = self.regions(k - 1)
            self.copy(k - 1, i).wait_recv()
            self.cur[i, pl.ds(keep, size)] += self.recvs[k - 1][i].astype(F32)
        size, _, away = self.regions(k)
        self.sends[k][i] = self.cur[i, pl.ds(away, size)].astype(BF16)
        self.copy(k, i).start()

    def result(self, i):
        self.copy(self.stages - 1, i).wait_recv()
        return self.cur[i, self.place] + self.recvs[-1][i, 0].astype(F32)

    def finish(self, count):
        for k in range(self.stages):
            for i in range(count):
                self.copy(k, i).wait_send()


def layer_kernel(
    s,
    pos_ref, len_ref, freq_ref, x_hbm, wq_hbm, wo_hbm, kc_hbm, vc_hbm,
    out_ref,
    x_v, wq_v, wo_v, kc_v, vc_v,
    qcur, qsend, qrecv, heads_v, acc, psend, precv, qs, os,
    x_sem, kv_sem, wq_sem, wo_sem,
    qsend_sem, qrecv_sem, gsend_sem, grecv_sem, psend_sem, precv_sem,
):
    nw, nn = s["nw"], s["nn"]
    H, G, HD = s["H"], s["G"], s["HD"]
    R = s["R"]
    C, NC, B = s["C"], s["NC"], s["B"]
    C2, NP = s["C2"], s["NP"]
    HK = G * HD
    GP = s["GP"]
    slots = s["slots"]
    q = nw // nn
    total = H * NC
    pieces = H * NP
    scale = HD ** -0.5
    me = lax.axis_index("wide")
    qsum = Halving("wide", nw, qcur, qsend, qrecv, qsend_sem, qrecv_sem)
    psum = Halving("narrow", nn, acc, psend, precv, psend_sem, precv_sem)
    SW, SN, LAG = qsum.stages, psum.stages, 2

    def wq_copy(i):
        slot = lax.rem(i, B)
        return pltpu.make_async_copy(
            wq_hbm.at[:, pl.ds(pl.multiple_of(i * C, C), C)], wq_v.at[slot], wq_sem.at[slot]
        )

    def wo_copy(i):
        h, c = i // NP, lax.rem(i, NP)
        return pltpu.make_async_copy(
            wo_hbm.at[pl.ds(pl.multiple_of(h * HK, HK), HK), pl.ds(pl.multiple_of(c * C2, C2), C2)],
            wo_v.at[i],
            wo_sem.at[i],
        )

    x_copy = pltpu.make_async_copy(x_hbm, x_v, x_sem)
    k_copy = pltpu.make_async_copy(kc_hbm, kc_v, kv_sem.at[0])
    v_copy = pltpu.make_async_copy(vc_hbm, vc_v, kv_sem.at[1])
    x_copy.start()
    for i in range(B):
        wq_copy(jnp.int32(i)).start()
    k_copy.start()
    v_copy.start()

    barrier = pltpu.get_barrier_semaphore()
    for part in (qsum, psum):
        for k in range(part.stages):
            pl.semaphore_signal(
                barrier, inc=1, device_id={part.axis: part.partner(k)}, device_id_type=MESH
            )

    row_id = lax.broadcasted_iota(jnp.int32, (R, HD), 0)
    place = jnp.zeros((R, HD), jnp.int32)
    for r in range(R):
        place = jnp.where(row_id == r, pos_ref[r], place)
    freq = jnp.broadcast_to(freq_ref[...], (R, HD))
    lane = lax.broadcasted_iota(jnp.int32, (2 * R, HD), 1)
    angles = jnp.concatenate([place.astype(F32) * freq, (place + 1).astype(F32) * freq], axis=0)
    cosine = jnp.cos(angles)
    sine = jnp.sin(angles)
    sine = jnp.where(lane < HD // 2, -sine, sine)
    qs[...] = jnp.zeros_like(qs)

    pl.semaphore_wait(barrier, SW + SN)
    x_copy.wait()

    def chunk(i):
        wq_copy(i).wait()
        slot = lax.rem(i, B)
        got = jnp.dot(
            x_v[...].reshape(2 * nw * R, x_v.shape[-1]), wq_v[slot], preferred_element_type=F32
        )
        half = nw * R
        for p in range(nw):
            qcur[i, reversed_bits(p, nw)] = jnp.concatenate(
                [got[p * R:(p + 1) * R], got[half + p * R:half + (p + 1) * R]], axis=0
            )
        qsum.exchange(0, i)

        @pl.when(i + B < total)
        def _():
            wq_copy(i + B).start()

        @pl.when((i + B >= total) & (i + B - total < pieces))
        def _():
            wo_copy(i + B - total).start()

    def chunks(lo, hi):
        def body(i, carry):
            @pl.when(i < total)
            def _():
                chunk(i)

            for k in range(1, SW):

                @pl.when((i >= k * LAG) & (i < total + k * LAG))
                def _():
                    qsum.exchange(k, i - k * LAG)

            return carry

        lax.fori_loop(lo, hi, body, 0)

    def attention(h):
        joined = [qsum.result(h * NC + c) for c in range(NC)]
        per = C // HD

        def entry(g):
            return joined[g // per][:, (g % per) * HD:(g % per + 1) * HD]

        def rotated(g):
            t = entry(g)
            t = t * cosine + pltpu.roll(t, HD // 2, 1) * sine
            return t.astype(BF16).astype(F32)

        for g in range(G):
            t = rotated(g)
            qs[:, g, :] = t[:R]
            qs[:, GP + g, :] = t[R:]
        key_new = rotated(G)
        value_new = entry(G + 1).astype(BF16).astype(F32)
        slot_id = lax.broadcasted_iota(jnp.int32, (2 * GP, slots), 1)
        second = lax.broadcasted_iota(jnp.int32, (2 * GP, 1), 0) >= GP
        for r in range(R):
            qr = qs[r]
            scores = lax.dot_general(
                qr.astype(BF16), kc_v[r, h], (((1,), (1,)), ((), ())), preferred_element_type=F32
            ) * scale
            e = jnp.where(slot_id < len_ref[r], jnp.exp(scores), 0.0)
            f0 = jnp.exp(jnp.sum(qr * key_new[r:r + 1], axis=1, keepdims=True) * scale)
            f1 = jnp.exp(jnp.sum(qr * key_new[R + r:R + r + 1], axis=1, keepdims=True) * scale)
            f1 = jnp.where(second, f1, 0.0)
            den = jnp.sum(e, axis=1, keepdims=True) + f0 + f1
            o = jnp.dot((e / den).astype(BF16), vc_v[r, h], preferred_element_type=F32)
            o = o + (f0 / den).astype(BF16).astype(F32) * value_new[r:r + 1]
            o = o + (f1 / den).astype(BF16).astype(F32) * value_new[R + r:R + r + 1]
            os[r] = o
        for g in range(G):
            heads_v[h, qsum.place, :, g * HD:(g + 1) * HD] = jnp.concatenate(
                [os[:, g, :], os[:, GP + g, :]], axis=0
            ).astype(BF16)
        gather(h, 0)

    def gather_copy(h, j):
        k = SW - 1 - j
        size, keep, _ = qsum.regions(k)
        return pltpu.make_async_remote_copy(
            src_ref=heads_v.at[h, pl.ds(keep, size)],
            dst_ref=heads_v.at[h, pl.ds(keep, size)],
            send_sem=gsend_sem.at[h, j],
            recv_sem=grecv_sem.at[h, j],
            device_id={"wide": qsum.partner(k)},
            device_id_type=MESH,
        )

    def gather_wait(h, j):
        size, _, away = qsum.regions(SW - 1 - j)
        landed = heads_v.at[h, pl.ds(away, size)]
        pltpu.make_async_copy(landed, landed, grecv_sem.at[h, j]).wait()

    def gather(h, j):
        if j > 0:
            gather_wait(h, j - 1)
        gather_copy(h, j).start()

    def project(h, lo, hi):
        def piece(c):
            i = h * NP + c
            wo_copy(i).wait()
            got = jnp.dot(
                heads_v[h].reshape(nw * 2 * R, HK), wo_v[i], preferred_element_type=F32
            )
            for n in range(nn):
                block = jnp.concatenate(
                    [
                        got[reversed_bits(p, nw) * 2 * R:(reversed_bits(p, nw) + 1) * 2 * R]
                        for p in range(n * q, (n + 1) * q)
                    ],
                    axis=0,
                )
                at = reversed_bits(n, nn)
                acc[c, at] = acc[c, at] + block if h > 0 else block
            if h == H - 1:
                psum.exchange(0, c)

        def body(c, carry):
            @pl.when(c < NP)
            def _():
                piece(c)

            if h == H - 1:
                for k in range(1, SN):

                    @pl.when((c >= k * LAG) & (c < NP + k * LAG))
                    def _():
                        psum.exchange(k, c - k * LAG)

            return carry

        lax.fori_loop(lo, hi, body, 0)

    early = LAG * (SW - 1) + 3 <= NC
    done = 0
    end = total + LAG * (SW - 1)
    if early:
        for h in range(1, H):
            upto = h * NC + LAG * (SW - 1) + 3
            chunks(done, upto)
            done = upto
            if h == 1:
                k_copy.wait()
                v_copy.wait()
            attention(h - 1)
    chunks(done, end)
    for i in range(min(B, pieces), pieces):
        wo_copy(jnp.int32(i)).start()
    if not early or H == 1:
        k_copy.wait()
        v_copy.wait()
    for h in range(H - 1):
        if not early:
            attention(h)
        for j in range(1, SW):
            gather(h, j)
    attention(H - 1)
    for h in range(H - 1):
        gather_wait(h, SW - 1)
        mid = NP // 2 if h == H - 2 else NP
        project(h, 0, mid)
    for j in range(1, SW):
        gather(H - 1, j)
    if H > 1:
        project(H - 2, NP // 2, NP)
    gather_wait(H - 1, SW - 1)
    project(H - 1, 0, NP + LAG * (SN - 1))

    for c in range(NP):
        tot = psum.result(c)
        for t in range(2):
            part = jnp.concatenate(
                [tot[(2 * k + t) * R:(2 * k + t + 1) * R] for k in range(q)], axis=0
            )
            out_ref[t, :, c * C2:(c + 1) * C2] = part.astype(BF16)

    qsum.finish(total)
    psum.finish(NP)
    for h in range(H):
        for j in range(SW):
            gather_copy(h, j).wait_send()


def on_device(nw, nn, inputs, w_qkv, w_out, key_cache, value_cache, positions, lengths):
    R, H, slots, HD = key_cache.shape
    G = w_qkv.shape[1] // (H * HD) - 2
    K = w_qkv.shape[0]
    N = w_out.shape[1]
    HK = G * HD
    C = 2 * HD
    NC = w_qkv.shape[1] // (H * C)
    C2 = min(N, 4 * HD)
    NP = N // C2
    B = min(8, H * NC)
    GP = -(-G // 8) * 8
    q = nw // nn
    s = dict(nw=nw, nn=nn, H=H, G=G, HD=HD, R=R, C=C, NC=NC, B=B, C2=C2, NP=NP, GP=GP, slots=slots)
    half = np.arange(HD // 2, dtype=np.float64)
    freq = (500000.0 ** (-2.0 * half / HD)).astype(np.float32)
    freq = jnp.asarray(np.concatenate([freq, freq])[None, :])
    rows = q * 2 * R
    SW, SN = nw.bit_length() - 1, nn.bit_length() - 1
    qbufs = [pltpu.VMEM((H * NC, nw // 2 ** (k + 1), 2 * R, C), BF16) for k in range(SW)]
    pbufs = [pltpu.VMEM((NP, nn // 2 ** (k + 1), rows, C2), BF16) for k in range(SN)]
    any_spec = pl.BlockSpec(memory_space=pl.ANY)
    smem = pl.BlockSpec(memory_space=pltpu.SMEM)
    vmem = pl.BlockSpec(memory_space=pltpu.VMEM)
    dma = pltpu.SemaphoreType.DMA
    return pl.pallas_call(
        functools.partial(layer_kernel, s),
        out_shape=jax.ShapeDtypeStruct((2, q * R, N), BF16),
        in_specs=[smem, smem, vmem] + [any_spec] * 5,
        out_specs=vmem,
        scratch_shapes=[
            pltpu.VMEM(inputs.shape, BF16),
            pltpu.VMEM((B, K, C), BF16),
            pltpu.VMEM((H * NP, HK, C2), BF16),
            pltpu.VMEM(key_cache.shape, BF16),
            pltpu.VMEM(value_cache.shape, BF16),
            pltpu.VMEM((H * NC, nw, 2 * R, C), F32),
            qbufs,
            qbufs,
            pltpu.VMEM((H, nw, 2 * R, HK), BF16),
            pltpu.VMEM((NP, nn, rows, C2), F32),
            pbufs,
            pbufs,
            pltpu.VMEM((R, 2 * GP, HD), F32),
            pltpu.VMEM((R, 2 * GP, HD), F32),
            dma,
            dma((2,)),
            dma((B,)),
            dma((H * NP,)),
            dma((SW, H * NC)),
            dma((SW, H * NC)),
            dma((H, SW)),
            dma((H, SW)),
            dma((SN, NP)),
            dma((SN, NP)),
        ],
        compiler_params=pltpu.CompilerParams(
            collective_id=0, has_side_effects=True, vmem_limit_bytes=58 * 1024 * 1024
        ),
        cost_estimate=pl.CostEstimate(
            flops=4 * nw * R * (K * w_qkv.shape[1] + H * HK * N),
            bytes_accessed=2 * (w_qkv.size + w_out.size + 2 * key_cache.size),
            transcendentals=0,
        ),
    )(positions, lengths, freq, inputs, w_qkv, w_out, key_cache, value_cache)


def solution(mesh):
    placed = (
        P(None, "groups", "wide"),
        P("wide", "narrow"),
        P("narrow", "wide"),
        P(("groups", "wide"), "narrow", None, None),
        P(("groups", "wide"), "narrow", None, None),
        P(("groups", "wide")),
        P(("groups", "wide")),
    )
    return jax.shard_map(
        functools.partial(on_device, mesh.shape["wide"], mesh.shape["narrow"]),
        mesh=mesh,
        in_specs=placed,
        out_specs=P(None, ("groups", "narrow"), "wide"),
        check_vma=False,
    )
```

```python
import functools

import jax
import jax.numpy as jnp
import numpy as np
from jax import lax
from jax.experimental import pallas as pl
from jax.experimental.pallas import tpu as pltpu
from jax.sharding import PartitionSpec as P

MESH = pl.DeviceIdType.MESH
F32 = jnp.float32
BF16 = jnp.bfloat16


def layer_kernel(
    s,
    pos_ref, len_ref, freq_ref, x_hbm, wq_hbm, wo_hbm, kc_hbm, vc_hbm,
    out_ref,
    x_v, wq_v, wo_v, kc_v, vc_v,
    qsend, qrecv, heads_v, acc, psend, precv, qs, os,
    x_sem, kv_sem, wq_sem, wo_sem,
    qsend_sem, qrecv_sem, gsend_sem, grecv_sem, psend_sem, precv_sem,
):
    nw, nn = s["nw"], s["nn"]
    H, G, HD = s["H"], s["G"], s["HD"]
    R = s["R"]
    C, NC, B = s["C"], s["NC"], s["B"]
    C2, NP = s["C2"], s["NP"]
    HK = G * HD
    GP = s["GP"]
    slots = s["slots"]
    q = nw // nn
    total = H * NC
    pieces = H * NP
    scale = HD ** -0.5
    me = lax.axis_index("wide")
    me_n = lax.axis_index("narrow")

    def wide_at(d):
        return lax.rem(me + d, nw)

    def narrow_at(d):
        return lax.rem(me_n + d, nn)

    def wq_copy(i):
        slot = lax.rem(i, B)
        return pltpu.make_async_copy(
            wq_hbm.at[:, pl.ds(pl.multiple_of(i * C, C), C)], wq_v.at[slot], wq_sem.at[slot]
        )

    def wo_copy(i):
        h, c = i // NP, lax.rem(i, NP)
        return pltpu.make_async_copy(
            wo_hbm.at[pl.ds(pl.multiple_of(h * HK, HK), HK), pl.ds(pl.multiple_of(c * C2, C2), C2)],
            wo_v.at[i],
            wo_sem.at[i],
        )

    x_copy = pltpu.make_async_copy(x_hbm, x_v, x_sem)
    k_copy = pltpu.make_async_copy(kc_hbm, kc_v, kv_sem.at[0])
    v_copy = pltpu.make_async_copy(vc_hbm, vc_v, kv_sem.at[1])
    x_copy.start()
    for i in range(B):
        wq_copy(jnp.int32(i)).start()
    k_copy.start()
    v_copy.start()

    barrier = pltpu.get_barrier_semaphore()
    for d in range(1, nw):
        pl.semaphore_signal(barrier, inc=1, device_id={"wide": wide_at(d)}, device_id_type=MESH)
    for d in range(1, nn):
        pl.semaphore_signal(barrier, inc=1, device_id={"narrow": narrow_at(d)}, device_id_type=MESH)

    row_id = lax.broadcasted_iota(jnp.int32, (R, HD), 0)
    place = jnp.zeros((R, HD), jnp.int32)
    for r in range(R):
        place = jnp.where(row_id == r, pos_ref[r], place)
    freq = jnp.broadcast_to(freq_ref[...], (R, HD))
    lane = lax.broadcasted_iota(jnp.int32, (2 * R, HD), 1)
    angles = jnp.concatenate([place.astype(F32) * freq, (place + 1).astype(F32) * freq], axis=0)
    cosine = jnp.cos(angles)
    sine = jnp.sin(angles)
    sine = jnp.where(lane < HD // 2, -sine, sine)
    qs[...] = jnp.zeros_like(qs)

    pl.semaphore_wait(barrier, nw + nn - 2)
    x_copy.wait()

    def chunk(i, h):
        c = i - h * NC
        wq_copy(i).wait()
        slot = lax.rem(i, B)
        got = jnp.dot(
            x_v[...].reshape(2 * nw * R, x_v.shape[-1]), wq_v[slot], preferred_element_type=F32
        )
        half = nw * R
        for p in range(nw):
            qsend[h, p, c] = jnp.concatenate(
                [got[p * R:(p + 1) * R], got[half + p * R:half + (p + 1) * R]], axis=0
            ).astype(BF16)
        for d in range(nw - 1, 0, -1):
            to = wide_at(d)
            pltpu.make_async_remote_copy(
                src_ref=qsend.at[h, to, c],
                dst_ref=qrecv.at[h, me, c],
                send_sem=qsend_sem.at[h, d],
                recv_sem=qrecv_sem.at[h, d],
                device_id={"wide": to},
                device_id_type=MESH,
            ).start()

        @pl.when(i + B < total)
        def _():
            wq_copy(i + B).start()

        @pl.when((i + B >= total) & (i + B - total < pieces))
        def _():
            wo_copy(i + B - total).start()

    def chunks(h, lo, hi):
        def body(i, carry):
            chunk(i, h)
            return carry

        lax.fori_loop(h * NC + lo, h * NC + hi, body, 0)

    def attention(h):
        joined = qsend[h, me].astype(F32)
        for d in range(1, nw):
            src = lax.rem(me + nw - d, nw)
            pltpu.make_async_copy(qrecv.at[h, src], qrecv.at[h, src], qrecv_sem.at[h, d]).wait()
            joined = joined + qrecv[h, src].astype(F32)
        per = C // HD

        def entry(g):
            return joined[g // per][:, (g % per) * HD:(g % per + 1) * HD]

        def rotated(g):
            t = entry(g)
            t = t * cosine + pltpu.roll(t, HD // 2, 1) * sine
            return t.astype(BF16).astype(F32)

        for g in range(G):
            t = rotated(g)
            qs[:, g, :] = t[:R]
            qs[:, GP + g, :] = t[R:]
        key_new = rotated(G)
        value_new = entry(G + 1).astype(BF16).astype(F32)
        slot_id = lax.broadcasted_iota(jnp.int32, (2 * GP, slots), 1)
        second = lax.broadcasted_iota(jnp.int32, (2 * GP, 1), 0) >= GP
        for r in range(R):
            qr = qs[r]
            scores = lax.dot_general(
                qr.astype(BF16), kc_v[r, h], (((1,), (1,)), ((), ())), preferred_element_type=F32
            ) * scale
            e = jnp.where(slot_id < len_ref[r], jnp.exp(scores), 0.0)
            f0 = jnp.exp(jnp.sum(qr * key_new[r:r + 1], axis=1, keepdims=True) * scale)
            f1 = jnp.exp(jnp.sum(qr * key_new[R + r:R + r + 1], axis=1, keepdims=True) * scale)
            f1 = jnp.where(second, f1, 0.0)
            den = jnp.sum(e, axis=1, keepdims=True) + f0 + f1
            o = jnp.dot((e / den).astype(BF16), vc_v[r, h], preferred_element_type=F32)
            o = o + (f0 / den).astype(BF16).astype(F32) * value_new[r:r + 1]
            o = o + (f1 / den).astype(BF16).astype(F32) * value_new[R + r:R + r + 1]
            os[r] = o
        for g in range(G):
            heads_v[h, me, :, g * HD:(g + 1) * HD] = jnp.concatenate(
                [os[:, g, :], os[:, GP + g, :]], axis=0
            ).astype(BF16)
        for d in range(1, nw):
            pltpu.make_async_remote_copy(
                src_ref=heads_v.at[h, me],
                dst_ref=heads_v.at[h, me],
                send_sem=gsend_sem.at[h, d],
                recv_sem=grecv_sem.at[h, d],
                device_id={"wide": wide_at(d)},
                device_id_type=MESH,
            ).start()

    def project(h):
        for d in range(1, nw):
            src = lax.rem(me + nw - d, nw)
            pltpu.make_async_copy(heads_v.at[h, src], heads_v.at[h, src], grecv_sem.at[h, d]).wait()

        def body(c, carry):
            i = h * NP + c
            wo_copy(i).wait()
            got = jnp.dot(
                heads_v[h].reshape(nw * 2 * R, HK), wo_v[i], preferred_element_type=F32
            )
            if h > 0:
                got = got + acc[c]
            if h < H - 1:
                acc[c] = got
                return carry
            rows = q * 2 * R
            for n in range(nn):
                psend[n, c] = got[n * rows:(n + 1) * rows].astype(BF16)
            for d in range(1, nn):
                to = narrow_at(d)
                pltpu.make_async_remote_copy(
                    src_ref=psend.at[to, c],
                    dst_ref=precv.at[me_n, c],
                    send_sem=psend_sem.at[d],
                    recv_sem=precv_sem.at[d],
                    device_id={"narrow": to},
                    device_id_type=MESH,
                ).start()
            return carry

        lax.fori_loop(0, NP, body, 0)

    for h in range(H):
        cut = NC
        chunks(h, 0, cut)
        if h > 0:
            if h == 1:
                k_copy.wait()
                v_copy.wait()
            attention(h - 1)
            chunks(h, cut, NC)
    if H == 1:
        k_copy.wait()
        v_copy.wait()
    for i in range(min(B, pieces), pieces):
        wo_copy(jnp.int32(i)).start()
    attention(H - 1)
    for h in range(H):
        project(h)

    for d in range(1, nn):
        src = lax.rem(me_n + nn - d, nn)
        pltpu.make_async_copy(precv.at[src], precv.at[src], precv_sem.at[d]).wait()
    for c in range(NP):
        tot = psend[me_n, c].astype(F32)
        for d in range(1, nn):
            tot = tot + precv[narrow_at(d), c].astype(F32)
        for t in range(2):
            part = jnp.concatenate(
                [tot[(2 * k + t) * R:(2 * k + t + 1) * R] for k in range(q)], axis=0
            )
            out_ref[t, :, c * C2:(c + 1) * C2] = part.astype(BF16)

    for d in range(1, nw):
        for h in range(H):
            to = wide_at(d)
            pltpu.make_async_copy(qsend.at[h, to], qsend.at[h, to], qsend_sem.at[h, d]).wait()
            pltpu.make_async_copy(heads_v.at[h, me], heads_v.at[h, me], gsend_sem.at[h, d]).wait()
    for d in range(1, nn):
        to = narrow_at(d)
        pltpu.make_async_copy(psend.at[to], psend.at[to], psend_sem.at[d]).wait()


def on_device(nw, nn, inputs, w_qkv, w_out, key_cache, value_cache, positions, lengths):
    R, H, slots, HD = key_cache.shape
    G = w_qkv.shape[1] // (H * HD) - 2
    K = w_qkv.shape[0]
    N = w_out.shape[1]
    HK = G * HD
    C = 2 * HD
    NC = w_qkv.shape[1] // (H * C)
    C2 = min(N, 4 * HD)
    NP = N // C2
    B = min(8, H * NC)
    GP = -(-G // 8) * 8
    q = nw // nn
    s = dict(nw=nw, nn=nn, H=H, G=G, HD=HD, R=R, C=C, NC=NC, B=B, C2=C2, NP=NP, GP=GP, slots=slots)
    half = np.arange(HD // 2, dtype=np.float64)
    freq = (500000.0 ** (-2.0 * half / HD)).astype(np.float32)
    freq = jnp.asarray(np.concatenate([freq, freq])[None, :])
    rows = q * 2 * R
    any_spec = pl.BlockSpec(memory_space=pl.ANY)
    smem = pl.BlockSpec(memory_space=pltpu.SMEM)
    vmem = pl.BlockSpec(memory_space=pltpu.VMEM)
    dma = pltpu.SemaphoreType.DMA
    return pl.pallas_call(
        functools.partial(layer_kernel, s),
        out_shape=jax.ShapeDtypeStruct((2, q * R, N), BF16),
        in_specs=[smem, smem, vmem] + [any_spec] * 5,
        out_specs=vmem,
        scratch_shapes=[
            pltpu.VMEM(inputs.shape, BF16),
            pltpu.VMEM((B, K, C), BF16),
            pltpu.VMEM((H * NP, HK, C2), BF16),
            pltpu.VMEM(key_cache.shape, BF16),
            pltpu.VMEM(value_cache.shape, BF16),
            pltpu.VMEM((H, nw, NC, 2 * R, C), BF16),
            pltpu.VMEM((H, nw, NC, 2 * R, C), BF16),
            pltpu.VMEM((H, nw, 2 * R, HK), BF16),
            pltpu.VMEM((NP, nw * 2 * R, C2), F32),
            pltpu.VMEM((nn, NP, rows, C2), BF16),
            pltpu.VMEM((nn, NP, rows, C2), BF16),
            pltpu.VMEM((R, 2 * GP, HD), F32),
            pltpu.VMEM((R, 2 * GP, HD), F32),
            dma,
            dma((2,)),
            dma((B,)),
            dma((H * NP,)),
            dma((H, nw)),
            dma((H, nw)),
            dma((H, nw)),
            dma((H, nw)),
            dma((nn,)),
            dma((nn,)),
        ],
        compiler_params=pltpu.CompilerParams(
            collective_id=0, has_side_effects=True, vmem_limit_bytes=58 * 1024 * 1024
        ),
        cost_estimate=pl.CostEstimate(
            flops=4 * nw * R * (K * w_qkv.shape[1] + H * HK * N),
            bytes_accessed=2 * (w_qkv.size + w_out.size + 2 * key_cache.size),
            transcendentals=0,
        ),
    )(positions, lengths, freq, inputs, w_qkv, w_out, key_cache, value_cache)


def solution(mesh):
    placed = (
        P(None, "groups", "wide"),
        P("wide", "narrow"),
        P("narrow", "wide"),
        P(("groups", "wide"), "narrow", None, None),
        P(("groups", "wide"), "narrow", None, None),
        P(("groups", "wide")),
        P(("groups", "wide")),
    )
    return jax.shard_map(
        functools.partial(on_device, mesh.shape["wide"], mesh.shape["narrow"]),
        mesh=mesh,
        in_specs=placed,
        out_specs=P(None, ("groups", "narrow"), "wide"),
        check_vma=False,
    )
```

```python
import functools

import jax
import jax.numpy as jnp
import numpy as np
from jax import lax
from jax.experimental import pallas as pl
from jax.experimental.pallas import tpu as pltpu
from jax.sharding import PartitionSpec as P

MESH = pl.DeviceIdType.MESH
F32 = jnp.float32
BF16 = jnp.bfloat16


def layer_kernel(
    s,
    pos_ref, len_ref, freq_ref, x_hbm, wq_hbm, wo_hbm, kc_hbm, vc_hbm,
    out_ref,
    x_v, wq_v, wo_v, kc_v, vc_v,
    qsend, qrecv, heads_v, acc, psend, precv, qs, os,
    x_sem, kv_sem, wq_sem, wo_sem,
    qsend_sem, qrecv_sem, gsend_sem, grecv_sem, psend_sem, precv_sem,
):
    nw, nn = s["nw"], s["nn"]
    H, G, HD = s["H"], s["G"], s["HD"]
    R = s["R"]
    C, NC, B = s["C"], s["NC"], s["B"]
    C2, NP = s["C2"], s["NP"]
    HK = G * HD
    GP = s["GP"]
    slots = s["slots"]
    q = nw // nn
    total = H * NC
    pieces = H * NP
    scale = HD ** -0.5
    me = lax.axis_index("wide")
    me_n = lax.axis_index("narrow")

    def wide_at(d):
        return lax.rem(me + d, nw)

    def narrow_at(d):
        return lax.rem(me_n + d, nn)

    def wq_copy(i):
        slot = lax.rem(i, B)
        return pltpu.make_async_copy(
            wq_hbm.at[:, pl.ds(pl.multiple_of(i * C, C), C)], wq_v.at[slot], wq_sem.at[slot]
        )

    def wo_copy(i):
        h, c = i // NP, lax.rem(i, NP)
        return pltpu.make_async_copy(
            wo_hbm.at[pl.ds(pl.multiple_of(h * HK, HK), HK), pl.ds(pl.multiple_of(c * C2, C2), C2)],
            wo_v.at[i],
            wo_sem.at[i],
        )

    x_copy = pltpu.make_async_copy(x_hbm, x_v, x_sem)
    k_copy = pltpu.make_async_copy(kc_hbm, kc_v, kv_sem.at[0])
    v_copy = pltpu.make_async_copy(vc_hbm, vc_v, kv_sem.at[1])
    x_copy.start()
    for i in range(B):
        wq_copy(jnp.int32(i)).start()
    k_copy.start()
    v_copy.start()

    barrier = pltpu.get_barrier_semaphore()
    for d in range(1, nw):
        pl.semaphore_signal(barrier, inc=1, device_id={"wide": wide_at(d)}, device_id_type=MESH)
    for d in range(1, nn):
        pl.semaphore_signal(barrier, inc=1, device_id={"narrow": narrow_at(d)}, device_id_type=MESH)

    row_id = lax.broadcasted_iota(jnp.int32, (R, HD), 0)
    place = jnp.zeros((R, HD), jnp.int32)
    for r in range(R):
        place = jnp.where(row_id == r, pos_ref[r], place)
    freq = jnp.broadcast_to(freq_ref[...], (R, HD))
    lane = lax.broadcasted_iota(jnp.int32, (2 * R, HD), 1)
    angles = jnp.concatenate([place.astype(F32) * freq, (place + 1).astype(F32) * freq], axis=0)
    cosine = jnp.cos(angles)
    sine = jnp.sin(angles)
    sine = jnp.where(lane < HD // 2, -sine, sine)
    qs[...] = jnp.zeros_like(qs)

    pl.semaphore_wait(barrier, nw + nn - 2)
    x_copy.wait()

    def chunk(i, h):
        c = i - h * NC
        wq_copy(i).wait()
        slot = lax.rem(i, B)
        got = jnp.dot(
            x_v[...].reshape(2 * nw * R, x_v.shape[-1]), wq_v[slot], preferred_element_type=F32
        )
        half = nw * R
        for p in range(nw):
            qsend[h, p, c] = jnp.concatenate(
                [got[p * R:(p + 1) * R], got[half + p * R:half + (p + 1) * R]], axis=0
            ).astype(BF16)
        for d in range(nw - 1, 0, -1):
            to = wide_at(d)
            pltpu.make_async_remote_copy(
                src_ref=qsend.at[h, to, c],
                dst_ref=qrecv.at[h, me, c],
                send_sem=qsend_sem.at[h, d],
                recv_sem=qrecv_sem.at[h, d],
                device_id={"wide": to},
                device_id_type=MESH,
            ).start()

        @pl.when(i + B < total)
        def _():
            wq_copy(i + B).start()

        @pl.when((i + B >= total) & (i + B - total < pieces))
        def _():
            wo_copy(i + B - total).start()

    def chunks(h, lo, hi):
        def body(i, carry):
            chunk(i, h)
            return carry

        lax.fori_loop(h * NC + lo, h * NC + hi, body, 0)

    def attention(h):
        joined = qsend[h, me].astype(F32)
        for d in range(1, nw):
            src = lax.rem(me + nw - d, nw)
            pltpu.make_async_copy(qrecv.at[h, src], qrecv.at[h, src], qrecv_sem.at[h, d]).wait()
            joined = joined + qrecv[h, src].astype(F32)
        per = C // HD

        def entry(g):
            return joined[g // per][:, (g % per) * HD:(g % per + 1) * HD]

        def rotated(g):
            t = entry(g)
            t = t * cosine + pltpu.roll(t, HD // 2, 1) * sine
            return t.astype(BF16).astype(F32)

        for g in range(G):
            t = rotated(g)
            qs[:, g, :] = t[:R]
            qs[:, GP + g, :] = t[R:]
        key_new = rotated(G)
        value_new = entry(G + 1).astype(BF16).astype(F32)
        slot_id = lax.broadcasted_iota(jnp.int32, (2 * GP, slots), 1)
        second = lax.broadcasted_iota(jnp.int32, (2 * GP, 1), 0) >= GP
        for r in range(R):
            qr = qs[r]
            scores = lax.dot_general(
                qr.astype(BF16), kc_v[r, h], (((1,), (1,)), ((), ())), preferred_element_type=F32
            ) * scale
            e = jnp.where(slot_id < len_ref[r], jnp.exp(scores), 0.0)
            f0 = jnp.exp(jnp.sum(qr * key_new[r:r + 1], axis=1, keepdims=True) * scale)
            f1 = jnp.exp(jnp.sum(qr * key_new[R + r:R + r + 1], axis=1, keepdims=True) * scale)
            f1 = jnp.where(second, f1, 0.0)
            den = jnp.sum(e, axis=1, keepdims=True) + f0 + f1
            o = jnp.dot((e / den).astype(BF16), vc_v[r, h], preferred_element_type=F32)
            o = o + (f0 / den).astype(BF16).astype(F32) * value_new[r:r + 1]
            o = o + (f1 / den).astype(BF16).astype(F32) * value_new[R + r:R + r + 1]
            os[r] = o
        for g in range(G):
            heads_v[h, me, :, g * HD:(g + 1) * HD] = jnp.concatenate(
                [os[:, g, :], os[:, GP + g, :]], axis=0
            ).astype(BF16)
        for d in range(1, nw):
            pltpu.make_async_remote_copy(
                src_ref=heads_v.at[h, me],
                dst_ref=heads_v.at[h, me],
                send_sem=gsend_sem.at[h, d],
                recv_sem=grecv_sem.at[h, d],
                device_id={"wide": wide_at(d)},
                device_id_type=MESH,
            ).start()

    def project(h):
        for d in range(1, nw):
            src = lax.rem(me + nw - d, nw)
            pltpu.make_async_copy(heads_v.at[h, src], heads_v.at[h, src], grecv_sem.at[h, d]).wait()

        def body(c, carry):
            i = h * NP + c
            wo_copy(i).wait()
            got = jnp.dot(
                heads_v[h].reshape(nw * 2 * R, HK), wo_v[i], preferred_element_type=F32
            )
            if h > 0:
                got = got + acc[c]
            if h < H - 1:
                acc[c] = got
                return carry
            rows = q * 2 * R
            for n in range(nn):
                psend[n, c] = got[n * rows:(n + 1) * rows].astype(BF16)
            for d in range(1, nn):
                to = narrow_at(d)
                pltpu.make_async_remote_copy(
                    src_ref=psend.at[to, c],
                    dst_ref=precv.at[me_n, c],
                    send_sem=psend_sem.at[d],
                    recv_sem=precv_sem.at[d],
                    device_id={"narrow": to},
                    device_id_type=MESH,
                ).start()
            return carry

        lax.fori_loop(0, NP, body, 0)

    for h in range(H):
        cut = NC
        chunks(h, 0, cut)
        if h == H - 1:
            for i in range(min(B, pieces), pieces):
                wo_copy(jnp.int32(i)).start()
        if h > 0:
            if h == 1:
                k_copy.wait()
                v_copy.wait()
            attention(h - 1)
            chunks(h, cut, NC)
    if H == 1:
        k_copy.wait()
        v_copy.wait()
    attention(H - 1)
    for h in range(H):
        project(h)

    for d in range(1, nn):
        src = lax.rem(me_n + nn - d, nn)
        pltpu.make_async_copy(precv.at[src], precv.at[src], precv_sem.at[d]).wait()
    for c in range(NP):
        tot = psend[me_n, c].astype(F32)
        for d in range(1, nn):
            tot = tot + precv[narrow_at(d), c].astype(F32)
        for t in range(2):
            part = jnp.concatenate(
                [tot[(2 * k + t) * R:(2 * k + t + 1) * R] for k in range(q)], axis=0
            )
            out_ref[t, :, c * C2:(c + 1) * C2] = part.astype(BF16)

    for d in range(1, nw):
        for h in range(H):
            to = wide_at(d)
            pltpu.make_async_copy(qsend.at[h, to], qsend.at[h, to], qsend_sem.at[h, d]).wait()
            pltpu.make_async_copy(heads_v.at[h, me], heads_v.at[h, me], gsend_sem.at[h, d]).wait()
    for d in range(1, nn):
        to = narrow_at(d)
        pltpu.make_async_copy(psend.at[to], psend.at[to], psend_sem.at[d]).wait()


def on_device(nw, nn, inputs, w_qkv, w_out, key_cache, value_cache, positions, lengths):
    R, H, slots, HD = key_cache.shape
    G = w_qkv.shape[1] // (H * HD) - 2
    K = w_qkv.shape[0]
    N = w_out.shape[1]
    HK = G * HD
    C = 2 * HD
    NC = w_qkv.shape[1] // (H * C)
    C2 = min(N, 8 * HD)
    NP = N // C2
    B = min(8, H * NC)
    GP = -(-G // 8) * 8
    q = nw // nn
    s = dict(nw=nw, nn=nn, H=H, G=G, HD=HD, R=R, C=C, NC=NC, B=B, C2=C2, NP=NP, GP=GP, slots=slots)
    half = np.arange(HD // 2, dtype=np.float64)
    freq = (500000.0 ** (-2.0 * half / HD)).astype(np.float32)
    freq = jnp.asarray(np.concatenate([freq, freq])[None, :])
    rows = q * 2 * R
    any_spec = pl.BlockSpec(memory_space=pl.ANY)
    smem = pl.BlockSpec(memory_space=pltpu.SMEM)
    vmem = pl.BlockSpec(memory_space=pltpu.VMEM)
    dma = pltpu.SemaphoreType.DMA
    return pl.pallas_call(
        functools.partial(layer_kernel, s),
        out_shape=jax.ShapeDtypeStruct((2, q * R, N), BF16),
        in_specs=[smem, smem, vmem] + [any_spec] * 5,
        out_specs=vmem,
        scratch_shapes=[
            pltpu.VMEM(inputs.shape, BF16),
            pltpu.VMEM((B, K, C), BF16),
            pltpu.VMEM((H * NP, HK, C2), BF16),
            pltpu.VMEM(key_cache.shape, BF16),
            pltpu.VMEM(value_cache.shape, BF16),
            pltpu.VMEM((H, nw, NC, 2 * R, C), BF16),
            pltpu.VMEM((H, nw, NC, 2 * R, C), BF16),
            pltpu.VMEM((H, nw, 2 * R, HK), BF16),
            pltpu.VMEM((NP, nw * 2 * R, C2), F32),
            pltpu.VMEM((nn, NP, rows, C2), BF16),
            pltpu.VMEM((nn, NP, rows, C2), BF16),
            pltpu.VMEM((R, 2 * GP, HD), F32),
            pltpu.VMEM((R, 2 * GP, HD), F32),
            dma,
            dma((2,)),
            dma((B,)),
            dma((H * NP,)),
            dma((H, nw)),
            dma((H, nw)),
            dma((H, nw)),
            dma((H, nw)),
            dma((nn,)),
            dma((nn,)),
        ],
        compiler_params=pltpu.CompilerParams(
            collective_id=0, has_side_effects=True, vmem_limit_bytes=58 * 1024 * 1024
        ),
        cost_estimate=pl.CostEstimate(
            flops=4 * nw * R * (K * w_qkv.shape[1] + H * HK * N),
            bytes_accessed=2 * (w_qkv.size + w_out.size + 2 * key_cache.size),
            transcendentals=0,
        ),
    )(positions, lengths, freq, inputs, w_qkv, w_out, key_cache, value_cache)


def solution(mesh):
    placed = (
        P(None, "groups", "wide"),
        P("wide", "narrow"),
        P("narrow", "wide"),
        P(("groups", "wide"), "narrow", None, None),
        P(("groups", "wide"), "narrow", None, None),
        P(("groups", "wide")),
        P(("groups", "wide")),
    )
    return jax.shard_map(
        functools.partial(on_device, mesh.shape["wide"], mesh.shape["narrow"]),
        mesh=mesh,
        in_specs=placed,
        out_specs=P(None, ("groups", "narrow"), "wide"),
        check_vma=False,
    )
```
